32 devices in a mesh: rep: 2 (over y), seg: 16 (over z, x, core).
Axes of the slice: x: 2, y: 2, z: 4, core: 2. Of those that a mesh axis runs over, the one named last changes fastest.
Arguments:
- initial: bfloat16 [32, 256, 128], P('rep'), parts along dimension 0, may hold values from -6 to 6
- left_env: bfloat16 [96, 16, 256, 256], P(('rep', 'seg')), parts along dimension 0, may hold values from -0.375 to 0.375
- partner_right: bfloat16 [96, 16, 128, 128], P(('rep', 'seg')), parts along dimension 0, may hold values from -0.5 to 0.5
- term_coef: float32 [96], P(('rep', 'seg')), parts along dimension 0, may hold values from 0.02 to 0.2
- term_source: int32 [96, 16], P('rep'), parts along dimension 0, may hold values from 0 to 15
- sector_rows: int32 [32], P('rep'), parts along dimension 0, may hold values from 64 to 256, as said below
Outputs:
- last_image: bfloat16 [8192, 128], P(('rep', 'seg')), parts along dimension 0
- projected: float32 [6, 3], P('rep'), parts along dimension 0
The draws below stay inside these ranges and needn't reach their ends.
There are 2 independent parts, one for each index of `rep`. The reference program is written for one: setup_inputs(seed, part) draws one part's arguments, and reference() takes and returns one part's arrays. A program takes and returns all parts, laid end to end along the dimension named above; each array names one. Nothing has to cross between parts.
Inputs may be any that keep to these rules, and one draw needn't show every extreme that they name: `sector_rows`: every value is a multiple of 64, and at least one block has exactly 256 live rows.
All inputs are finite; a program needn't handle non-finite values.
Results may differ from the reference program's by a relative error of at most 0.0095.
Values may be sent and summed in bfloat16 or wider, within the bound.
A program may use at most 64 MiB of HBM per device.

```python
import math
import jax
import jax.numpy as jnp
from jax import lax

SECT = 16
TILE = 64
BL = 256
BR = 128
TERM_DEV = 3
MATVECS = 3
TERMS = 48


def draw_sector_rows(key, part):
    key = jax.random.fold_in(key, 7)
    first_key, second_key = jax.random.split(key)
    tiles = jax.random.randint(first_key, (SECT,), 1, 5)
    chosen = jax.random.randint(second_key, (), 0, SECT)
    tiles = jnp.where(jnp.arange(SECT) == chosen, 4, tiles)
    return (tiles * TILE).astype(jnp.int32)


def set_ends(drawn, key, smallest, largest):
    spot = [jax.random.randint(jax.random.fold_in(key, axis), (), 0, length) for axis, length in enumerate(drawn.shape)]
    main_axis = drawn.shape.index(max(drawn.shape))
    next_to = spot[:main_axis] + [(spot[main_axis] + 1) % drawn.shape[main_axis]] + spot[main_axis + 1:]
    return drawn.at[tuple(spot)].set(smallest).at[tuple(next_to)].set(largest)


def block_scale(key, shape, cuts, smallest, largest):
    level = 1.0
    for dim, blocks in cuts:
        draws = jax.random.uniform(jax.random.fold_in(jax.random.fold_in(key, 6), dim), (blocks,), jnp.float32, smallest / len(cuts), largest / len(cuts))
        level = level * jnp.repeat(jnp.exp(draws), shape[dim] // blocks).reshape((-1,) + (1,) * (len(shape) - 1 - dim))
    return level


def scatter_about(key, dims, scale, limit, pieces=(), held_as=jnp.bfloat16):
    array = scale * jax.random.normal(key, dims, jnp.float32)
    if pieces:
        array = array * block_scale(key, dims, pieces, -0.22, 0.18)
    return jnp.clip(array, -limit, limit).astype(held_as)


def setup_inputs(seed: int = 0, part: int = 0) -> dict:
    seeds = jax.random.split(jax.random.key(seed), 7)
    own_keys = jax.random.split(jax.random.fold_in(seeds[6], part), 7)
    initial = scatter_about(own_keys[0], (SECT, BL, BR), 1.0, 6.0)
    left_env = scatter_about(own_keys[1], (TERMS, SECT, BL, BL), BL ** -0.5, 0.375, ((0, 16),))
    partner_right = scatter_about(own_keys[2], (TERMS, SECT, BR, BR), BR ** -0.5, 0.5, ((0, 16),))
    term_coef = jnp.clip(jnp.exp(math.log(0.2) - 2.3025851 * jax.random.uniform(own_keys[3], (TERMS,), jnp.float32) ** block_scale(own_keys[3], (TERMS,), ((0, 16),), -0.2, 0.2)), 0.02, 0.2)
    term_source = set_ends(jax.random.randint(own_keys[4], (TERMS, SECT), 0, SECT), jax.random.fold_in(own_keys[4], 1), 0, SECT - 1).astype(jnp.int32)
    sector_rows = draw_sector_rows(jax.random.fold_in(jax.random.fold_in(seeds[6], part), 71), part)
    return dict(initial=initial, left_env=left_env, partner_right=partner_right, term_coef=term_coef, term_source=term_source, sector_rows=sector_rows)


epsilon = 1e-06

def reference(initial, left_env, partner_right, term_coef, term_source, sector_rows):
    total_rows = SECT * BL
    entries = float(total_rows * BR)
    index = jnp.arange(TERMS, dtype=jnp.int32)
    mirror = (jnp.bitwise_xor(index // TERM_DEV, 1) * TERM_DEV + index % TERM_DEV).astype(jnp.int32)
    live = (lax.broadcasted_iota(jnp.int32, (SECT, BL), 1) < sector_rows[:, None]).astype(jnp.float32).reshape(total_rows, 1)

    def matvec(vector):
        blocks = vector.reshape(SECT, BL, BR).astype(jnp.float32)

        def advance(total, inputs):
            left, sources, coupling, slot = inputs
            right = partner_right[slot].astype(jnp.float32)
            moved = jnp.einsum('sab,scb->sac', blocks[sources], right, precision=lax.Precision.HIGHEST).astype(jnp.bfloat16)
            moved = lax.optimization_barrier(moved)
            term = jnp.einsum('sij,sjc->sic', left.astype(jnp.float32), moved.astype(jnp.float32), precision=lax.Precision.HIGHEST)
            return (total + coupling * term, None)
        total, _ = lax.scan(advance, jnp.zeros((SECT, BL, BR), jnp.float32), (left_env, term_source, term_coef, mirror))
        return total.reshape(total_rows, BR) * live
    start = initial.reshape(total_rows, BR).astype(jnp.float32) * live
    basis = [(start * lax.rsqrt(jnp.sum(start * start) / entries + epsilon)).astype(jnp.bfloat16)]
    images = []
    for step in range(MATVECS):
        image = matvec(basis[step])
        images.append(image)
        if step + 1 < MATVECS:
            residual = image
            for vector in basis:
                correlation = jnp.sum(vector.astype(jnp.float32) * image)
                residual = residual - correlation / entries * vector.astype(jnp.float32)
            scale = lax.rsqrt(jnp.sum(residual * residual) / entries + epsilon)
            basis.append((residual * scale).astype(jnp.bfloat16))
    values = [jnp.sum(vector.astype(jnp.float32) * image) for vector in basis for image in images]
    projected = jnp.stack(values).reshape(MATVECS, MATVECS) / entries
    return (images[-1].astype(jnp.bfloat16), projected)
```

```python
import functools

import jax
import jax.numpy as jnp
from jax import lax
from jax.experimental import pallas as pl
from jax.experimental.pallas import tpu as pltpu
from jax.sharding import PartitionSpec as P

MATVECS = 3
EPS = 1e-06
F32, BF16 = jnp.float32, jnp.bfloat16
MESH = pl.DeviceIdType.MESH


def bit_of(value, b):
    return lax.rem(lax.div(value, jnp.int32(2**b)), jnp.int32(2))


def orders_of(levels):
    natural = tuple(range(levels))
    if levels < 3:
        return (natural, natural)
    return (natural, (0,) + tuple(range(2, levels)) + (1,))


def place(block, order):
    levels = len(order)
    pos = 0
    for i, b in enumerate(order):
        pos = pos + bit_of(block, b) * 2 ** (levels - 1 - i)
    return pos


def kernel(
    n, levels, sectors, rows, cols, terms,
    source_ref, coef_ref, live_ref, initial_ref, left_hbm, right_hbm,
    image_ref, projected_ref,
    left, right, basis, partial_a, partial_b, gather_a, gather_b,
    first_a, first_b, send_a, send_b, recv_a, recv_b, sum_a, sum_b,
    dots_send, dots_recv,
    left_sem, right_send, right_recv,
    rs_send, rs_recv, ag_send, ag_recv, dot_send_sem, dot_recv_sem,
):
    me = lax.axis_index("seg")
    rep = lax.axis_index("rep")
    total = sectors * rows
    half = total // (2 * n)
    entries = float(total * cols)
    per_sector = max(1, n // sectors)
    orders = orders_of(levels)
    partial = (partial_a, partial_b)
    gathered = (gather_a, gather_b)
    first = (first_a, first_b)
    sends = (send_a, send_b)
    recvs = (recv_a, recv_b)
    sums = (sum_a, sum_b)

    def peer_of(b):
        return me + (1 - 2 * bit_of(me, b)) * 2**b

    def target(b):
        return (rep, peer_of(b))

    left_copy = pltpu.make_async_copy(left_hbm, left, left_sem)
    left_copy.start()

    barrier = pltpu.get_barrier_semaphore()
    for b in range(levels):
        pl.semaphore_signal(barrier, inc=1, device_id=target(b), device_id_type=MESH)
    pl.semaphore_wait(barrier, levels)

    right_copy = pltpu.make_async_remote_copy(
        right_hbm, right, right_send, right_recv, device_id=target(0), device_id_type=MESH
    )
    right_copy.start()

    def row_mask(s):
        return lax.broadcasted_iota(jnp.int32, (rows, cols), 0) < live_ref[s]

    def fold8(x):
        return jnp.sum(x.reshape(rows // 8, 8, cols), axis=0)

    def square_body(s, acc):
        x = jnp.where(row_mask(s), initial_ref[s].astype(F32), 0.0)
        return acc + fold8(x * x)

    squares = lax.fori_loop(0, sectors, square_body, jnp.zeros((8, cols), F32))
    start_scale = lax.rsqrt(jnp.sum(squares) / entries + EPS)

    def start_body(s, carry):
        x = jnp.where(row_mask(s), initial_ref[s].astype(F32), 0.0)
        basis[0, s] = (x * start_scale).astype(BF16)
        return carry

    lax.fori_loop(0, sectors, start_body, 0)

    left_copy.wait()
    right_copy.wait()

    scales = [jnp.float32(1.0)]
    values = {}
    for k in range(MATVECS):
        last = k == MATVECS - 1
        pairs = [(j, k) for j in range(k + 1)] + [(k, i) for i in range(k)]
        scale = scales[k]

        def sector_body(s, carry, k=k, pairs=pairs, scale=scale):
            acc = jnp.zeros((rows, cols), F32)
            for t in range(terms):
                src = source_ref[me * terms + t, s]
                block = basis[k, src]
                moved = lax.dot_general(
                    block, right[t, s], (((1,), (1,)), ((), ())), preferred_element_type=F32
                ).astype(BF16)
                acc = acc + coef_ref[t] * jnp.dot(left[t, s], moved, preferred_element_type=F32)
            acc = jnp.where(row_mask(s), acc * scale, 0.0)
            if n >= sectors:
                for i in range(per_sector):
                    block_id = s * per_sector + i
                    for p in range(2):
                        piece = acc[(2 * i + p) * half:(2 * i + p + 1) * half]
                        at = pl.ds(pl.multiple_of(place(block_id, orders[p]) * half, half), half)
                        partial[p][k, at, :] = piece
                        first[p][at, :] = piece.astype(BF16)
            out = []
            for (j, i), total_here in zip(pairs, carry):
                vec = basis[j, s].astype(F32)
                if i == k:
                    out.append(total_here + fold8(vec * acc))
                else:
                    for q in range(per_sector):
                        block_id = s * per_sector + q
                        for p in range(2):
                            at = pl.ds(pl.multiple_of(place(block_id, orders[p]) * half, half), half)
                            prod = vec[(2 * q + p) * half:(2 * q + p + 1) * half] * partial[p][i, at, :]
                            total_here = total_here + jnp.sum(prod.reshape(half // 8, 8, cols), axis=0)
                    out.append(total_here)
            return tuple(out)

        dots = lax.fori_loop(
            0, sectors, sector_body, tuple(jnp.zeros((8, cols), F32) for _ in pairs)
        )
        tile = jnp.concatenate(
            [jnp.sum(d, axis=0, keepdims=True) for d in dots]
            + [jnp.zeros((8 - len(pairs), cols), F32)],
            axis=0,
        )

        def rs_copy(p, i, k=k):
            b = orders[p][i]
            size = total // 2 // 2 ** (i + 1)
            if i == 0:
                start = (1 - bit_of(me, b)) * size
                src = first[p].at[pl.ds(pl.multiple_of(start, half), size), :]
            else:
                src = sends[p].at[pl.ds(offsets[i], size), :]
            return pltpu.make_async_remote_copy(
                src, recvs[p].at[k, pl.ds(offsets[i], size), :],
                rs_send.at[k, p, i], rs_recv.at[k, p, i],
                device_id=target(b), device_id_type=MESH,
            )

        def dot_copy(i, k=k):
            return pltpu.make_async_remote_copy(
                dots_send.at[k, i], dots_recv.at[k, i],
                dot_send_sem.at[k, i], dot_recv_sem.at[k, i],
                device_id=target(i), device_id_type=MESH,
            )

        offsets = [total // 2 - total // 2 // 2**i for i in range(levels + 1)]
        pending = [rs_copy(0, 0), rs_copy(1, 0)]
        dots_send[k, 0] = tile
        dot_pending = dot_copy(0)
        pending[0].start()
        pending[1].start()
        dot_pending.start()
        final = [None, None]
        for i in range(levels):
            for p in range(2):
                size = total // 2 // 2 ** (i + 1)
                b = orders[p][i]
                my = bit_of(me, b)

                def mine(begin, count, i=i, p=p, my=my, size=size, k=k):
                    at = pl.ds(pl.multiple_of(my * size + begin, half), count)
                    own = partial[p][k, at, :] if i == 0 else sums[p][
                        pl.ds(pl.multiple_of(offsets[i - 1] + my * size + begin, half), count), :]
                    other = recvs[p][k, pl.ds(pl.multiple_of(offsets[i] + begin, half), count), :]
                    return own + other.astype(F32)

                pending[p].wait()
                if i == levels - 1:
                    final[p] = mine(0, size)
                else:
                    child = size // 2
                    next_my = bit_of(me, orders[p][i + 1])
                    sends[p][pl.ds(offsets[i + 1], child), :] = mine((1 - next_my) * child, child).astype(BF16)
                    pending[p] = rs_copy(p, i + 1)
                    pending[p].start()
                    sums[p][pl.ds(pl.multiple_of(offsets[i] + next_my * child, half), child), :] = mine(next_my * child, child)
            dot_pending.wait()
            tile = tile + dots_recv[k, i]
            if i < levels - 1:
                dots_send[k, i + 1] = tile
                dot_pending = dot_copy(i + 1)
                dot_pending.start()
        for q, (j, i) in enumerate(pairs):
            values[j, i] = jnp.sum(tile[q:q + 1]) * (scales[j] / entries)
        if last:
            for p in range(2):
                image_ref[pl.ds(p * half, half), :] = final[p].astype(BF16)
            break

        ag_pending = [None, None]

        def ag_copy(p, i, k=k):
            size = total // 2 // 2 ** (i + 1)
            start = 0
            for level in range(i + 1):
                start = start + bit_of(me, orders[p][level]) * (total // 2 // 2 ** (level + 1))
            at = pl.ds(pl.multiple_of(start, half), size)
            return pltpu.make_async_remote_copy(
                gathered[p].at[k, at, :], gathered[p].at[k, at, :],
                ag_send.at[k, p, i], ag_recv.at[k, p, i],
                device_id=target(orders[p][i]), device_id_type=MESH,
            )

        for p in range(2):
            residual = final[p]
            own_sector = lax.div(me, per_sector)
            own_start = lax.rem(me, per_sector) * (2 * half) + p * half
            own_rows = pl.ds(pl.multiple_of(own_start, half), half)
            for j in range(k + 1):
                residual = residual - values[j, k] * scales[j] * basis[j, own_sector, own_rows, :].astype(F32)
            at = pl.ds(pl.multiple_of(place(me, orders[p]) * half, half), half)
            gathered[p][k, at, :] = residual.astype(BF16)
            ag_pending[p] = ag_copy(p, levels - 1)
            ag_pending[p].start()
        for i in reversed(range(levels)):
            for p in range(2):
                ag_pending[p].wait()
                if i > 0:
                    ag_pending[p] = ag_copy(p, i - 1)
                    ag_pending[p].start()

        def unpack_body(s, acc, k=k):
            for q in range(per_sector):
                block_id = s * per_sector + q
                for p in range(2):
                    at = pl.ds(pl.multiple_of(place(block_id, orders[p]) * half, half), half)
                    piece = gathered[p][k, at, :]
                    basis[k + 1, s, pl.ds((2 * q + p) * half, half), :] = piece
                    wide = piece.astype(F32)
                    acc = acc + jnp.sum((wide * wide).reshape(half // 8, 8, cols), axis=0)
            return acc

        squares = lax.fori_loop(0, sectors, unpack_body, jnp.zeros((8, cols), F32))
        scales.append(lax.rsqrt(jnp.sum(squares) / entries + EPS))

    for j in range(MATVECS):
        for i in range(MATVECS):
            projected_ref[j, i] = values[j, i]


def on_device(n, initial, left_env, partner_right, term_coef, term_source, sector_rows):
    sectors, rows, cols = initial.shape
    terms = left_env.shape[0]
    levels = n.bit_length() - 1
    total = sectors * rows
    part = total // 2
    vmem = pl.BlockSpec(memory_space=pltpu.VMEM)
    smem = pl.BlockSpec(memory_space=pltpu.SMEM)
    anym = pl.BlockSpec(memory_space=pl.ANY)
    dma = pltpu.SemaphoreType.DMA
    return pl.pallas_call(
        functools.partial(kernel, n, levels, sectors, rows, cols, terms),
        out_shape=(
            jax.ShapeDtypeStruct((total // n, cols), BF16),
            jax.ShapeDtypeStruct((MATVECS, MATVECS), F32),
        ),
        in_specs=[smem, smem, smem, vmem, anym, anym],
        out_specs=(vmem, smem),
        scratch_shapes=[
            pltpu.VMEM(left_env.shape, BF16),
            pltpu.VMEM(partner_right.shape, BF16),
            pltpu.VMEM((MATVECS, sectors, rows, cols), BF16),
            pltpu.VMEM((MATVECS, part, cols), F32),
            pltpu.VMEM((MATVECS, part, cols), F32),
            pltpu.VMEM((MATVECS - 1, part, cols), BF16),
            pltpu.VMEM((MATVECS - 1, part, cols), BF16),
            pltpu.VMEM((part, cols), BF16),
            pltpu.VMEM((part, cols), BF16),
            pltpu.VMEM((part, cols), BF16),
            pltpu.VMEM((part, cols), BF16),
            pltpu.VMEM((MATVECS, part, cols), BF16),
            pltpu.VMEM((MATVECS, part, cols), BF16),
            pltpu.VMEM((part, cols), F32),
            pltpu.VMEM((part, cols), F32),
            pltpu.VMEM((MATVECS, levels, 8, cols), F32),
            pltpu.VMEM((MATVECS, levels, 8, cols), F32),
            dma,
            dma,
            dma,
            dma((MATVECS, 2, levels)),
            dma((MATVECS, 2, levels)),
            dma((MATVECS, 2, levels)),
            dma((MATVECS, 2, levels)),
            dma((MATVECS, levels)),
            dma((MATVECS, levels)),
        ],
        compiler_params=pltpu.CompilerParams(
            collective_id=0, has_side_effects=True, vmem_limit_bytes=48 * 1024 * 1024
        ),
    )(term_source, term_coef, sector_rows, initial, left_env, partner_right)


def solution(mesh):
    return jax.shard_map(
        functools.partial(on_device, mesh.shape["seg"]),
        mesh=mesh,
        in_specs=(
            P("rep", None, None),
            P(("rep", "seg"), None, None, None),
            P(("rep", "seg"), None, None, None),
            P(("rep", "seg")),
            P("rep", None),
            P("rep"),
        ),
        out_specs=(P(("rep", "seg"), None), P("rep", None)),
        check_vma=False,
    )
```

```python
import functools

import jax
import jax.numpy as jnp
from jax import lax
from jax.experimental import pallas as pl
from jax.experimental.pallas import tpu as pltpu
from jax.sharding import PartitionSpec as P

MATVECS = 3
EPS = 1e-06
F32, BF16 = jnp.float32, jnp.bfloat16
MESH = pl.DeviceIdType.MESH


def bit_of(value, b):
    return lax.rem(lax.div(value, jnp.int32(2**b)), jnp.int32(2))


def stages_of(levels, parts):
    groups = [(b,) for b in range(min(2, levels))]
    groups += [tuple(range(b, min(b + 2, levels))) for b in range(2, levels, 2)]
    turned = groups[:1] + groups[2:] + groups[1:2]
    return [turned if p == parts - 2 else groups for p in range(parts)]


def dot_stages_of(levels):
    return [(0,)] + [tuple(range(b, min(b + 3, levels))) for b in range(1, levels, 3)]


def group_value(device, group):
    value = 0
    for i, b in enumerate(group):
        value = value + bit_of(device, b) * 2**i
    return value


def place(block, stages, levels):
    pos, room = 0, 2**levels
    for group in stages:
        room //= 2 ** len(group)
        pos = pos + group_value(block, group) * room
    return pos


def kernel(
    n, levels, parts, sectors, rows, cols, terms,
    source_ref, coef_ref, live_ref, initial_ref, left_hbm, right_hbm,
    image_ref, projected_ref,
    left, right, basis, partial, gathered, first, sends, recvs, sums, dots_all,
    left_sem, right_send, right_recv,
    rs_send, rs_recv, ag_send, ag_recv, dot_send_sem, dot_recv_sem,
):
    me = lax.axis_index("seg")
    rep = lax.axis_index("rep")
    total = sectors * rows
    part_rows = total // parts
    piece_rows = part_rows // n
    entries = float(total * cols)
    per_sector = max(1, n // sectors)
    stages = stages_of(levels, parts)
    dot_stages = dot_stages_of(levels)

    def peer(group, diff):
        other = me
        for i, b in enumerate(group):
            if diff >> i & 1:
                other = other + (1 - 2 * bit_of(me, b)) * 2**b
        return other

    def target(group, diff):
        return (rep, peer(group, diff))

    left_copy = pltpu.make_async_copy(left_hbm, left, left_sem)
    left_copy.start()

    partners = {}
    for group in [g for part in stages for g in part] + dot_stages:
        for diff in range(1, 2 ** len(group)):
            mask = sum(2**b for i, b in enumerate(group) if diff >> i & 1)
            partners[mask] = target(group, diff)
    barrier = pltpu.get_barrier_semaphore()
    for mask in sorted(partners):
        pl.semaphore_signal(barrier, inc=1, device_id=partners[mask], device_id_type=MESH)
    pl.semaphore_wait(barrier, len(partners))

    right_copy = pltpu.make_async_remote_copy(
        right_hbm, right, right_send, right_recv, device_id=target((0,), 1), device_id_type=MESH
    )
    right_copy.start()

    def row_mask(s):
        return lax.broadcasted_iota(jnp.int32, (rows, cols), 0) < live_ref[s]

    def fold8(x):
        return jnp.sum(x.reshape(x.shape[0] // 8, 8, cols), axis=0)

    def square_body(s, acc):
        x = jnp.where(row_mask(s), initial_ref[s].astype(F32), 0.0)
        return acc + fold8(x * x)

    squares = lax.fori_loop(0, sectors, square_body, jnp.zeros((8, cols), F32))
    start_scale = lax.rsqrt(jnp.sum(squares) / entries + EPS)

    def start_body(s, carry):
        x = jnp.where(row_mask(s), initial_ref[s].astype(F32), 0.0)
        basis[0, s] = (x * start_scale).astype(BF16)
        return carry

    lax.fori_loop(0, sectors, start_body, 0)

    left_copy.wait()
    right_copy.wait()

    plan = []
    for p in range(parts):
        size, offset, steps = part_rows, 0, []
        for group in stages[p]:
            members = 2 ** len(group)
            share = size // members
            steps.append((group, members, size, share, offset))
            offset += (members - 1) * share
            size = share
        plan.append(steps)
    count = [len(steps) for steps in plan]

    def piece_at(block_id, p):
        return pl.ds(pl.multiple_of(place(block_id, stages[p], levels) * piece_rows, piece_rows), piece_rows)

    def pieces_of(s):
        for q in range(per_sector):
            for p in range(parts):
                yield p, (q * parts + p) * piece_rows, piece_at(s * per_sector + q, p)

    scales = [jnp.float32(1.0)]
    values = {}
    for k in range(MATVECS):
        last = k == MATVECS - 1
        pairs = [(j, k) for j in range(k + 1)] + [(k, i) for i in range(k)]
        scale = scales[k]
        split = n == sectors

        def rs_copies(p, i, k=k):
            group, members, size, share, offset = plan[p][i]
            out = []
            for diff in range(1, members):
                slot = offset + (diff - 1) * share
                if i == 0:
                    start = group_value(peer(group, diff), group) * share
                    src = first.at[p, pl.ds(pl.multiple_of(start, piece_rows), share), :]
                else:
                    src = sends.at[p, pl.ds(slot, share), :]
                out.append(pltpu.make_async_remote_copy(
                    src, recvs.at[k, p, pl.ds(slot, share), :],
                    rs_send.at[k, p, i, diff - 1], rs_recv.at[k, p, i, diff - 1],
                    device_id=target(group, diff), device_id_type=MESH,
                ))
            return out

        def sector_body(i, carry, k=k, pairs=pairs, scale=scale, own=0):
            s = i * 2 + (bit_of(me, 0) if own else 1 - bit_of(me, 0)) if split else i
            acc = jnp.zeros((rows, cols), F32)
            for t in range(terms):
                src = source_ref[me * terms + t, s]
                moved = lax.dot_general(
                    basis[k, src], right[t, s], (((1,), (1,)), ((), ())), preferred_element_type=F32
                ).astype(BF16)
                acc = acc + coef_ref[t] * jnp.dot(left[t, s], moved, preferred_element_type=F32)
            acc = jnp.where(row_mask(s), acc * scale, 0.0)
            for p, begin, at in pieces_of(s):
                piece = acc[begin:begin + piece_rows]
                partial[k, p, at, :] = piece
                if not (split and own):
                    first[p, at, :] = piece.astype(BF16)
            out = []
            for (j, i2), so_far in zip(pairs, carry):
                vec = basis[j, s].astype(F32)
                if i2 == k:
                    so_far = so_far + fold8(vec * acc)
                else:
                    for p, begin, at in pieces_of(s):
                        so_far = so_far + fold8(vec[begin:begin + piece_rows] * partial[i2, p, at, :])
                out.append(so_far)
            return tuple(out)

        dots = tuple(jnp.zeros((8, cols), F32) for _ in pairs)
        started = []
        pending = [None] * parts
        if split:
            dots = lax.fori_loop(0, sectors // 2, functools.partial(sector_body, own=0), dots)
        else:
            dots = lax.fori_loop(0, sectors, sector_body, dots)
        for p in range(parts):
            pending[p] = rs_copies(p, 0)
            started += pending[p]
            for copy in pending[p]:
                copy.start()
        if split:
            dots = lax.fori_loop(0, sectors // 2, functools.partial(sector_body, own=1), dots)
        tile = jnp.concatenate(
            [jnp.sum(d, axis=0, keepdims=True) for d in dots]
            + [jnp.zeros((8 - len(pairs), cols), F32)],
            axis=0,
        )

        def dot_start(i, tile, k=k):
            group = dot_stages[i]
            dots_all[k, i, 0] = tile
            out = []
            for diff in range(1, 2 ** len(group)):
                out.append(pltpu.make_async_remote_copy(
                    dots_all.at[k, i, 0], dots_all.at[k, i, diff],
                    dot_send_sem.at[k, i, diff - 1], dot_recv_sem.at[k, i, diff - 1],
                    device_id=target(group, diff), device_id_type=MESH,
                ))
                out[-1].start()
            return out

        def dot_finish(i, copies, k=k):
            group = dot_stages[i]
            for copy in copies:
                copy.wait()
            sum_here = jnp.zeros((8, cols), F32)
            for value in range(2 ** len(group)):
                slot = 0
                for q, b in enumerate(group):
                    bit = value >> q & 1
                    slot = slot + (1 - bit_of(me, b) if bit else bit_of(me, b)) * 2**q
                sum_here = sum_here + dots_all[k, i, slot]
            return sum_here

        dot_pending = dot_start(0, tile)
        dot_next = 0
        final = [None] * parts
        for i in range(max(count)):
            for p in range(parts):
                group, members, size, share, offset = plan[p][i]
                my = group_value(me, group)

                def mine(begin, length, i=i, p=p, k=k, my=my, share=share, offset=offset, members=members):
                    at = pl.ds(pl.multiple_of(my * share + begin, piece_rows), length)
                    x = partial[k, p, at, :] if i == 0 else sums[p, i - 1, at, :]
                    for diff in range(1, members):
                        slot = pl.multiple_of(offset + (diff - 1) * share + begin, piece_rows)
                        x = x + recvs[k, p, pl.ds(slot, length), :].astype(F32)
                    return x

                for copy in pending[p]:
                    copy.wait_recv()
                if i == count[p] - 1:
                    final[p] = mine(0, share)
                    continue
                next_group, next_members, _, child, next_offset = plan[p][i + 1]
                pending[p] = rs_copies(p, i + 1)
                started += pending[p]
                for diff, copy in enumerate(pending[p], 1):
                    begin = group_value(peer(next_group, diff), next_group) * child
                    slot = next_offset + (diff - 1) * child
                    sends[p, pl.ds(slot, child), :] = mine(begin, child).astype(BF16)
                    copy.start()
                begin = group_value(me, next_group) * child
                sums[p, i, pl.ds(pl.multiple_of(begin, piece_rows), child), :] = mine(begin, child)
            if dot_next < len(dot_stages):
                tile = dot_finish(dot_next, dot_pending)
                dot_next += 1
                if dot_next < len(dot_stages):
                    dot_pending = dot_start(dot_next, tile)
        for q, (j, i) in enumerate(pairs):
            values[j, i] = jnp.sum(tile[q:q + 1]) * (scales[j] / entries)
        if last:
            for p in range(parts):
                image_ref[pl.ds(p * piece_rows, piece_rows), :] = final[p].astype(BF16)
            for copy in started:
                copy.wait_send()
            break

        def ag_copies(p, i, k=k):
            group, members, size, share, offset = plan[p][i]
            start = 0
            for level in range(i + 1):
                start = start + group_value(me, plan[p][level][0]) * plan[p][level][3]
            at = pl.ds(pl.multiple_of(start, piece_rows), share)
            out = []
            for diff in range(1, members):
                out.append(pltpu.make_async_remote_copy(
                    gathered.at[k, p, at, :], gathered.at[k, p, at, :],
                    ag_send.at[k, p, i, diff - 1], ag_recv.at[k, p, i, diff - 1],
                    device_id=target(group, diff), device_id_type=MESH,
                ))
                out[-1].start()
            return out

        own_sector = lax.div(me, per_sector)
        for p in range(parts):
            residual = final[p]
            own_start = lax.rem(me, per_sector) * (parts * piece_rows) + p * piece_rows
            own_rows = pl.ds(pl.multiple_of(own_start, piece_rows), piece_rows)
            for j in range(k + 1):
                residual = residual - values[j, k] * scales[j] * basis[j, own_sector, own_rows, :].astype(F32)
            gathered[k, p, piece_at(me, p), :] = residual.astype(BF16)
            pending[p] = ag_copies(p, count[p] - 1)
            started += pending[p]
        for i in reversed(range(max(count))):
            for p in range(parts):
                for copy in pending[p]:
                    copy.wait_recv()
                if i > 0:
                    pending[p] = ag_copies(p, i - 1)
                    started += pending[p]

        def unpack_body(s, acc, k=k):
            for p, begin, at in pieces_of(s):
                piece = gathered[k, p, at, :]
                basis[k + 1, s, pl.ds(begin, piece_rows), :] = piece
                wide = piece.astype(F32)
                acc = acc + fold8(wide * wide)
            return acc

        squares = lax.fori_loop(0, sectors, unpack_body, jnp.zeros((8, cols), F32))
        scales.append(lax.rsqrt(jnp.sum(squares) / entries + EPS))
        for copy in started:
            copy.wait_send()

    for j in range(MATVECS):
        for i in range(MATVECS):
            projected_ref[j, i] = values[j, i]


def on_device(n, initial, left_env, partner_right, term_coef, term_source, sector_rows):
    sectors, rows, cols = initial.shape
    terms = left_env.shape[0]
    levels = n.bit_length() - 1
    total = sectors * rows
    parts = max(2, min(4, total // (16 * n)))
    part = total // parts
    stage_count = len(stages_of(levels, parts)[0])
    dot_count = len(dot_stages_of(levels))
    vmem = pl.BlockSpec(memory_space=pltpu.VMEM)
    smem = pl.BlockSpec(memory_space=pltpu.SMEM)
    anym = pl.BlockSpec(memory_space=pl.ANY)
    dma = pltpu.SemaphoreType.DMA
    return pl.pallas_call(
        functools.partial(kernel, n, levels, parts, sectors, rows, cols, terms),
        out_shape=(
            jax.ShapeDtypeStruct((total // n, cols), BF16),
            jax.ShapeDtypeStruct((MATVECS, MATVECS), F32),
        ),
        in_specs=[smem, smem, smem, vmem, anym, anym],
        out_specs=(vmem, smem),
        scratch_shapes=[
            pltpu.VMEM(left_env.shape, BF16),
            pltpu.VMEM(partner_right.shape, BF16),
            pltpu.VMEM((MATVECS, sectors, rows, cols), BF16),
            pltpu.VMEM((MATVECS, parts, part, cols), F32),
            pltpu.VMEM((MATVECS - 1, parts, part, cols), BF16),
            pltpu.VMEM((parts, part, cols), BF16),
            pltpu.VMEM((parts, part, cols), BF16),
            pltpu.VMEM((MATVECS, parts, part, cols), BF16),
            pltpu.VMEM((parts, stage_count, part // 2, cols), F32),
            pltpu.VMEM((MATVECS, dot_count, 8, 8, cols), F32),
            dma,
            dma,
            dma,
            dma((MATVECS, parts, stage_count, 3)),
            dma((MATVECS, parts, stage_count, 3)),
            dma((MATVECS, parts, stage_count, 3)),
            dma((MATVECS, parts, stage_count, 3)),
            dma((MATVECS, dot_count, 7)),
            dma((MATVECS, dot_count, 7)),
        ],
        compiler_params=pltpu.CompilerParams(
            collective_id=0, has_side_effects=True, vmem_limit_bytes=48 * 1024 * 1024
        ),
    )(term_source, term_coef, sector_rows, initial, left_env, partner_right)


def solution(mesh):
    return jax.shard_map(
        functools.partial(on_device, mesh.shape["seg"]),
        mesh=mesh,
        in_specs=(
            P("rep", None, None),
            P(("rep", "seg"), None, None, None),
            P(("rep", "seg"), None, None, None),
            P(("rep", "seg")),
            P("rep", None),
            P("rep"),
        ),
        out_specs=(P(("rep", "seg"), None), P("rep", None)),
        check_vma=False,
    )
```

```python
import functools

import jax
import jax.numpy as jnp
from jax import lax
from jax.experimental import pallas as pl
from jax.experimental.pallas import tpu as pltpu
from jax.sharding import PartitionSpec as P

MATVECS = 3
GROUP = 8
EPS = 1e-06
F32, BF16 = jnp.float32, jnp.bfloat16
MESH = pl.DeviceIdType.MESH


def bit_of(value, b):
    return lax.rem(lax.div(value, jnp.int32(2**b)), jnp.int32(2))


def stages_of(levels, parts):
    groups = [(b,) for b in range(min(2, levels))]
    groups += [tuple(range(b, min(b + 2, levels))) for b in range(2, levels, 2)]
    turned = groups[:1] + groups[2:] + groups[1:2]
    return [turned if p == parts - 2 else groups for p in range(parts)]


def dot_stages_of(levels):
    return [(0,)] + [tuple(range(b, min(b + 3, levels))) for b in range(1, levels, 3)]


def group_value(device, group):
    value = 0
    for i, b in enumerate(group):
        value = value + bit_of(device, b) * 2**i
    return value


def place(block, stages, levels):
    pos, room = 0, 2**levels
    for group in stages:
        room //= 2 ** len(group)
        pos = pos + group_value(block, group) * room
    return pos


def kernel(
    n, levels, parts, sectors, rows, cols, terms,
    source_ref, coef_ref, live_ref, initial_ref, left_hbm, right_hbm,
    image_ref, projected_ref,
    left, right, basis, partial, gathered, first, sends, recvs, sums, dots_all,
    left_sem, right_send, right_recv,
    rs_send, rs_recv, ag_send, ag_recv, dot_send_sem, dot_recv_sem,
):
    me = lax.axis_index("seg")
    rep = lax.axis_index("rep")
    total = sectors * rows
    part_rows = total // parts
    piece_rows = part_rows // n
    entries = float(total * cols)
    per_sector = max(1, n // sectors)
    stages = stages_of(levels, parts)
    dot_stages = dot_stages_of(levels)

    def peer(group, diff):
        other = me
        for i, b in enumerate(group):
            if diff >> i & 1:
                other = other + (1 - 2 * bit_of(me, b)) * 2**b
        return other

    def target(group, diff):
        return (rep, peer(group, diff))

    left_copy = pltpu.make_async_copy(left_hbm, left, left_sem)
    left_copy.start()

    partners = {}
    for group in [g for part in stages for g in part] + dot_stages:
        for diff in range(1, 2 ** len(group)):
            mask = sum(2**b for i, b in enumerate(group) if diff >> i & 1)
            partners[mask] = target(group, diff)
    barrier = pltpu.get_barrier_semaphore()
    for mask in sorted(partners):
        pl.semaphore_signal(barrier, inc=1, device_id=partners[mask], device_id_type=MESH)
    pl.semaphore_wait(barrier, len(partners))

    right_copy = pltpu.make_async_remote_copy(
        right_hbm, right, right_send, right_recv, device_id=target((0,), 1), device_id_type=MESH
    )
    right_copy.start()

    def row_mask(s):
        return lax.broadcasted_iota(jnp.int32, (rows, cols), 0) < live_ref[s]

    def fold8(x):
        return jnp.sum(x.reshape(x.shape[0] // 8, 8, cols), axis=0)

    def square_body(s, acc):
        x = jnp.where(row_mask(s), initial_ref[s].astype(F32), 0.0)
        return acc + fold8(x * x)

    squares = lax.fori_loop(0, sectors, square_body, jnp.zeros((8, cols), F32), unroll=2)
    start_scale = lax.rsqrt(jnp.sum(squares) / entries + EPS)

    def start_body(s, carry):
        x = jnp.where(row_mask(s), initial_ref[s].astype(F32), 0.0)
        basis[0, s] = (x * start_scale).astype(BF16)
        return carry

    lax.fori_loop(0, sectors, start_body, 0, unroll=2)

    left_copy.wait()
    right_copy.wait()

    plan = []
    for p in range(parts):
        size, offset, steps = part_rows, 0, []
        for group in stages[p]:
            members = 2 ** len(group)
            share = size // members
            steps.append((group, members, size, share, offset))
            offset += (members - 1) * share
            size = share
        plan.append(steps)
    count = [len(steps) for steps in plan]

    def piece_at(block_id, p):
        return pl.ds(pl.multiple_of(place(block_id, stages[p], levels) * piece_rows, piece_rows), piece_rows)

    def pieces_of(s):
        for q in range(per_sector):
            for p in range(parts):
                yield p, (q * parts + p) * piece_rows, piece_at(s * per_sector + q, p)

    scales = [jnp.float32(1.0)]
    values = {}
    for k in range(MATVECS):
        last = k == MATVECS - 1
        pairs = [(j, k) for j in range(k + 1)] + [(k, i) for i in range(k)]
        scale = scales[k]
        split = n == sectors

        def rs_copies(p, i, k=k):
            group, members, size, share, offset = plan[p][i]
            out = []
            for diff in range(1, members):
                slot = offset + (diff - 1) * share
                if i == 0:
                    start = group_value(peer(group, diff), group) * share
                    src = first.at[p, pl.ds(pl.multiple_of(start, piece_rows), share), :]
                else:
                    src = sends.at[p, pl.ds(slot, share), :]
                out.append(pltpu.make_async_remote_copy(
                    src, recvs.at[k, p, pl.ds(slot, share), :],
                    rs_send.at[k, p, i, diff - 1], rs_recv.at[k, p, i, diff - 1],
                    device_id=target(group, diff), device_id_type=MESH,
                ))
            return out

        def image_of(s, k=k, scale=scale):
            acc = jnp.zeros((rows, cols), F32)
            for t in range(terms):
                src = source_ref[me * terms + t, s]
                moved = lax.dot_general(
                    basis[k, src], right[t, s], (((1,), (1,)), ((), ())), preferred_element_type=F32
                ).astype(BF16)
                acc = acc + coef_ref[t] * jnp.dot(left[t, s], moved, preferred_element_type=F32)
            return jnp.where(row_mask(s), acc * scale, 0.0)

        def sector_body(i, carry, k=k, pairs=pairs, own=0):
            at_once = [i * GROUP + u for u in range(GROUP)]
            if split:
                at_once = [x * 2 + (bit_of(me, 0) if own else 1 - bit_of(me, 0)) for x in at_once]
            accs = [image_of(s) for s in at_once]
            for s, acc in zip(at_once, accs):
                for p, begin, at in pieces_of(s):
                    piece = acc[begin:begin + piece_rows]
                    partial[k, p, at, :] = piece
                    if not (split and own):
                        first[p, at, :] = piece.astype(BF16)
                out = []
                for (j, i2), so_far in zip(pairs, carry):
                    vec = basis[j, s].astype(F32)
                    if i2 == k:
                        so_far = so_far + fold8(vec * acc)
                    else:
                        for p, begin, at in pieces_of(s):
                            so_far = so_far + fold8(vec[begin:begin + piece_rows] * partial[i2, p, at, :])
                    out.append(so_far)
                carry = tuple(out)
            return carry

        dots = tuple(jnp.zeros((8, cols), F32) for _ in pairs)
        started = []
        pending = [None] * parts
        if split:
            dots = lax.fori_loop(0, sectors // 2 // GROUP, functools.partial(sector_body, own=0), dots)
        else:
            dots = lax.fori_loop(0, sectors // GROUP, sector_body, dots)
        for p in range(parts):
            pending[p] = rs_copies(p, 0)
            started += pending[p]
            for copy in pending[p]:
                copy.start()
        if split:
            dots = lax.fori_loop(0, sectors // 2 // GROUP, functools.partial(sector_body, own=1), dots)
        tile = jnp.concatenate(
            [jnp.sum(d, axis=0, keepdims=True) for d in dots]
            + [jnp.zeros((8 - len(pairs), cols), F32)],
            axis=0,
        )

        def dot_start(i, tile, k=k):
            group = dot_stages[i]
            dots_all[k, i, 0] = tile
            out = []
            for diff in range(1, 2 ** len(group)):
                out.append(pltpu.make_async_remote_copy(
                    dots_all.at[k, i, 0], dots_all.at[k, i, diff],
                    dot_send_sem.at[k, i, diff - 1], dot_recv_sem.at[k, i, diff - 1],
                    device_id=target(group, diff), device_id_type=MESH,
                ))
                out[-1].start()
            return out

        def dot_finish(i, copies, k=k):
            group = dot_stages[i]
            for copy in copies:
                copy.wait()
            sum_here = jnp.zeros((8, cols), F32)
            for value in range(2 ** len(group)):
                slot = 0
                for q, b in enumerate(group):
                    bit = value >> q & 1
                    slot = slot + (1 - bit_of(me, b) if bit else bit_of(me, b)) * 2**q
                sum_here = sum_here + dots_all[k, i, slot]
            return sum_here

        dot_pending = dot_start(0, tile)
        dot_next = 0
        final = [None] * parts
        for i in range(max(count)):
            for p in range(parts):
                group, members, size, share, offset = plan[p][i]
                my = group_value(me, group)

                def mine(begin, length, i=i, p=p, k=k, my=my, share=share, offset=offset, members=members):
                    at = pl.ds(pl.multiple_of(my * share + begin, piece_rows), length)
                    x = partial[k, p, at, :] if i == 0 else sums[p, i - 1, at, :]
                    for diff in range(1, members):
                        slot = pl.multiple_of(offset + (diff - 1) * share + begin, piece_rows)
                        x = x + recvs[k, p, pl.ds(slot, length), :].astype(F32)
                    return x

                for copy in pending[p]:
                    copy.wait_recv()
                if i == count[p] - 1:
                    final[p] = mine(0, share)
                    continue
                next_group, next_members, _, child, next_offset = plan[p][i + 1]
                pending[p] = rs_copies(p, i + 1)
                started += pending[p]
                for diff, copy in enumerate(pending[p], 1):
                    begin = group_value(peer(next_group, diff), next_group) * child
                    slot = next_offset + (diff - 1) * child
                    sends[p, pl.ds(slot, child), :] = mine(begin, child).astype(BF16)
                    copy.start()
                begin = group_value(me, next_group) * child
                sums[p, i, pl.ds(pl.multiple_of(begin, piece_rows), child), :] = mine(begin, child)
            if dot_next < len(dot_stages):
                tile = dot_finish(dot_next, dot_pending)
                dot_next += 1
                if dot_next < len(dot_stages):
                    dot_pending = dot_start(dot_next, tile)
        for q, (j, i) in enumerate(pairs):
            values[j, i] = jnp.sum(tile[q:q + 1]) * (scales[j] / entries)
        if last:
            for p in range(parts):
                image_ref[pl.ds(p * piece_rows, piece_rows), :] = final[p].astype(BF16)
            for copy in started:
                copy.wait_send()
            break

        def ag_copies(p, i, k=k):
            group, members, size, share, offset = plan[p][i]
            start = 0
            for level in range(i + 1):
                start = start + group_value(me, plan[p][level][0]) * plan[p][level][3]
            at = pl.ds(pl.multiple_of(start, piece_rows), share)
            out = []
            for diff in range(1, members):
                out.append(pltpu.make_async_remote_copy(
                    gathered.at[k, p, at, :], gathered.at[k, p, at, :],
                    ag_send.at[k, p, i, diff - 1], ag_recv.at[k, p, i, diff - 1],
                    device_id=target(group, diff), device_id_type=MESH,
                ))
                out[-1].start()
            return out

        own_sector = lax.div(me, per_sector)
        for p in range(parts):
            residual = final[p]
            own_start = lax.rem(me, per_sector) * (parts * piece_rows) + p * piece_rows
            own_rows = pl.ds(pl.multiple_of(own_start, piece_rows), piece_rows)
            for j in range(k + 1):
                residual = residual - values[j, k] * scales[j] * basis[j, own_sector, own_rows, :].astype(F32)
            gathered[k, p, piece_at(me, p), :] = residual.astype(BF16)
            pending[p] = ag_copies(p, count[p] - 1)
            started += pending[p]
        for i in reversed(range(max(count))):
            for p in range(parts):
                for copy in pending[p]:
                    copy.wait_recv()
                if i > 0:
                    pending[p] = ag_copies(p, i - 1)
                    started += pending[p]

        def unpack_body(s, acc, k=k):
            for p, begin, at in pieces_of(s):
                piece = gathered[k, p, at, :]
                basis[k + 1, s, pl.ds(begin, piece_rows), :] = piece
                wide = piece.astype(F32)
                acc = acc + fold8(wide * wide)
            return acc

        squares = lax.fori_loop(0, sectors, unpack_body, jnp.zeros((8, cols), F32), unroll=2)
        scales.append(lax.rsqrt(jnp.sum(squares) / entries + EPS))
        for copy in started:
            copy.wait_send()

    for j in range(MATVECS):
        for i in range(MATVECS):
            projected_ref[j, i] = values[j, i]


def on_device(n, initial, left_env, partner_right, term_coef, term_source, sector_rows):
    sectors, rows, cols = initial.shape
    terms = left_env.shape[0]
    levels = n.bit_length() - 1
    total = sectors * rows
    parts = max(2, min(4, total // (16 * n)))
    part = total // parts
    stage_count = len(stages_of(levels, parts)[0])
    dot_count = len(dot_stages_of(levels))
    vmem = pl.BlockSpec(memory_space=pltpu.VMEM)
    smem = pl.BlockSpec(memory_space=pltpu.SMEM)
    anym = pl.BlockSpec(memory_space=pl.ANY)
    dma = pltpu.SemaphoreType.DMA
    return pl.pallas_call(
        functools.partial(kernel, n, levels, parts, sectors, rows, cols, terms),
        out_shape=(
            jax.ShapeDtypeStruct((total // n, cols), BF16),
            jax.ShapeDtypeStruct((MATVECS, MATVECS), F32),
        ),
        in_specs=[smem, smem, smem, vmem, anym, anym],
        out_specs=(vmem, smem),
        scratch_shapes=[
            pltpu.VMEM(left_env.shape, BF16),
            pltpu.VMEM(partner_right.shape, BF16),
            pltpu.VMEM((MATVECS, sectors, rows, cols), BF16),
            pltpu.VMEM((MATVECS, parts, part, cols), F32),
            pltpu.VMEM((MATVECS - 1, parts, part, cols), BF16),
            pltpu.VMEM((parts, part, cols), BF16),
            pltpu.VMEM((parts, part, cols), BF16),
            pltpu.VMEM((MATVECS, parts, part, cols), BF16),
            pltpu.VMEM((parts, stage_count, part // 2, cols), F32),
            pltpu.VMEM((MATVECS, dot_count, 8, 8, cols), F32),
            dma,
            dma,
            dma,
            dma((MATVECS, parts, stage_count, 3)),
            dma((MATVECS, parts, stage_count, 3)),
            dma((MATVECS, parts, stage_count, 3)),
            dma((MATVECS, parts, stage_count, 3)),
            dma((MATVECS, dot_count, 7)),
            dma((MATVECS, dot_count, 7)),
        ],
        compiler_params=pltpu.CompilerParams(
            collective_id=0, has_side_effects=True, vmem_limit_bytes=48 * 1024 * 1024
        ),
    )(term_source, term_coef, sector_rows, initial, left_env, partner_right)


def solution(mesh):
    return jax.shard_map(
        functools.partial(on_device, mesh.shape["seg"]),
        mesh=mesh,
        in_specs=(
            P("rep", None, None),
            P(("rep", "seg"), None, None, None),
            P(("rep", "seg"), None, None, None),
            P(("rep", "seg")),
            P("rep", None),
            P("rep"),
        ),
        out_specs=(P(("rep", "seg"), None), P("rep", None)),
        check_vma=False,
    )
```
